128 devices in a mesh: node: 16 (over y, x), local: 8 (over z, core).
Axes of the slice: x: 4, y: 4, z: 4, core: 2. Of those that a mesh axis runs over, the one named last changes fastest.
Arguments:
- moe_in: bfloat16 [2048, 3584], P(('node', 'local')), may hold values from -6 to 6
- route_ids: int32 [2048, 8], P(('node', 'local')), may hold values from 0 to 127, as said below
- route_weights: float32 [2048, 8], P(('node', 'local')), may hold values from 0.05 to 0.6
- w_gate: bfloat16 [128, 3584, 1024], P(('node', 'local')), may hold values from -0.09375 to 0.09375
- w_up: bfloat16 [128, 3584, 1024], P(('node', 'local')), may hold values from -0.09375 to 0.09375
- w_down: bfloat16 [128, 1024, 3584], P(('node', 'local')), may hold values from -0.1875 to 0.1875
- queries: bfloat16 [128, 128, 576], P(('node', 'local')), may hold values from -70 to 70
- cache_latent: bfloat16 [128, 2048, 512], P(('node', 'local')), may hold values from -12 to 12
- cache_rope: bfloat16 [128, 64, 2048], P(('node', 'local')), may hold values from -2 to 2
- lengths: int32 [128], P(('node', 'local')), may hold values from 256 to 2048, as said below
Outputs:
- moe_out: bfloat16 [2048, 3584], P(('node', 'local'))
- attn_out: bfloat16 [128, 128, 512], P(('node', 'local'))
The draws below stay inside these ranges and needn't reach their ends.
Inputs may be any that keep to these rules, and one draw needn't show every extreme that they name: `route_ids`: each row names 8 different experts, 2 in each of 4 different node groups; expert e lies in node group e // 8 and is held by the device of flat index e (node major). Within the rows of one device (aligned blocks of 16 rows) no node group is used by more than 8 rows and no expert is named by more than 2 rows; in every such block some node group is used by exactly 8 rows and each of its experts is named by exactly 2 rows. `lengths`: at least one row has all 2048 slots filled.
All inputs are finite; a program needn't handle non-finite values.
Results may differ from the reference program's by a relative error of at most 0.012.
Values may be sent and summed in bfloat16 or wider, within the bound.
No kernel may reach another device: no remote copies, remote signals or barrier semaphores. Data moves between devices by JAX's collectives and lax.ppermute only.
A program may use at most 128 MiB of HBM per device.

```python
import math
import jax
import jax.numpy as jnp
from jax import lax

D = 3584
H = 1024
HEADS = 128
KV_RANK = 512
ROPE = 64
TOPK = 8
TOPG = 4
ROWS_DEV = 16
CACHE = 2048
GROUPS = 16
GROUP_EXPERTS = 8
EXPERTS = 128
SOURCES = 128
NODE_CAP = 8
TOKENS = 2048
ATT_ROWS = 128


def draw_queries(key, part):
    key = jax.random.fold_in(key, 21)
    values = jnp.clip(0.5 * jax.random.normal(key, (ATT_ROWS, HEADS, KV_RANK + ROPE), jnp.float32), -3.0, 3.0)
    return values.astype(jnp.bfloat16)


def draw_cache_latent(key, part):
    key = jax.random.fold_in(key, 22)
    value_key, scale_key = jax.random.split(key)
    spread = jnp.exp(jax.random.uniform(scale_key, (ATT_ROWS, CACHE, 1), jnp.float32, jnp.log(0.3), jnp.log(3.0)))
    values = jnp.clip(jax.random.normal(value_key, (ATT_ROWS, CACHE, KV_RANK), jnp.float32), -4.0, 4.0) * spread
    return values.astype(jnp.bfloat16)


def draw_cache_rope(key, part):
    key = jax.random.fold_in(key, 23)
    values = jnp.clip(0.5 * jax.random.normal(key, (ATT_ROWS, ROPE, CACHE), jnp.float32), -2.0, 2.0)
    return values.astype(jnp.bfloat16)


def draw_lengths(key, part):
    key = jax.random.fold_in(key, 24)
    first_key, second_key = jax.random.split(key)
    drawn = jax.random.randint(first_key, (ATT_ROWS,), CACHE // 8, CACHE + 1, dtype=jnp.int32)
    full_row = jax.random.randint(second_key, (), 0, ATT_ROWS, dtype=jnp.int32)
    return jnp.where(jnp.arange(ATT_ROWS, dtype=jnp.int32) == full_row, CACHE, drawn).astype(jnp.int32)


def draw_route_ids(key, part):
    key = jax.random.fold_in(key, 25)
    keys = jax.random.split(key, 7)
    group_index = jnp.arange(GROUPS, dtype=jnp.int32)
    hot_group = jax.random.randint(keys[0], (), 0, GROUPS, dtype=jnp.int32)
    hot_offset = jax.random.randint(keys[1], (), 0, GROUP_EXPERTS, dtype=jnp.int32)
    row_noise = jax.random.randint(keys[2], (SOURCES, ROWS_DEV), 0, 4096, dtype=jnp.int32)
    row_score = row_noise * ROWS_DEV + jnp.arange(ROWS_DEV, dtype=jnp.int32)[None, :]
    hot_rows = lax.top_k(row_score, NODE_CAP)[1].astype(jnp.int32)
    row_ids = jnp.arange(ROWS_DEV, dtype=jnp.int32)
    has_hot = jnp.sum((hot_rows[:, None, :] == row_ids[None, :, None]).astype(jnp.int32), axis=-1, dtype=jnp.int32)
    group_noise = jax.random.randint(keys[3], (SOURCES, GROUPS), 0, 4096, dtype=jnp.int32)
    is_hot_group = (group_index == hot_group)[None, :]
    group_score = jnp.where(is_hot_group, 8192 * GROUPS, group_noise * GROUPS + group_index[None, :])
    order = lax.top_k(group_score, GROUPS)[1].astype(jnp.int32)
    others = order[:, 1:]
    other_count = TOPG - has_hot
    other_start = jnp.cumsum(other_count, axis=1, dtype=jnp.int32) - other_count
    slot_index = jnp.arange(TOPG, dtype=jnp.int32)[None, None, :]
    take_at = (other_start[:, :, None] + slot_index - has_hot[:, :, None] + (GROUPS - 1)) % (GROUPS - 1)
    others_wide = jnp.broadcast_to(others[:, None, :], (SOURCES, ROWS_DEV, GROUPS - 1))
    picked = jnp.take_along_axis(others_wide, take_at, axis=2)
    chosen_groups = jnp.where((has_hot[:, :, None] == 1) & (slot_index == 0), hot_group, picked).astype(jnp.int32)
    member = jnp.sum((chosen_groups[..., None] == group_index).astype(jnp.int32), axis=-2, dtype=jnp.int32)
    earlier = jnp.cumsum(member, axis=1, dtype=jnp.int32) - member
    is_hot = (group_index == hot_group)[None, None, :]
    offsets = jax.random.randint(keys[6], (SOURCES, 1, GROUPS), 0, GROUP_EXPERTS, dtype=jnp.int32)
    offsets = jnp.broadcast_to(jnp.where(is_hot, hot_offset, offsets), (SOURCES, ROWS_DEV, GROUPS))
    rank_in = jnp.take_along_axis(earlier, chosen_groups, axis=2)
    start_at = jnp.take_along_axis(offsets, chosen_groups, axis=2)
    pair_size = TOPK // TOPG
    within = (start_at[..., None] + pair_size * rank_in[..., None] + jnp.arange(pair_size, dtype=jnp.int32)) % GROUP_EXPERTS
    chosen = chosen_groups[..., None] * GROUP_EXPERTS + within
    return chosen.reshape(TOKENS, TOPK).astype(jnp.int32)


def steps_of(stream_key, extent, cuts, low, top_value):
    def one(dim, shards_of):
        steps = jax.random.uniform(jax.random.fold_in(jax.random.fold_in(stream_key, 6), dim), (shards_of,), jnp.float32, low / len(cuts), top_value / len(cuts))
        return jnp.repeat(jnp.exp(steps), extent[dim] // shards_of).reshape((-1,) + (1,) * (len(extent) - dim - 1))

    level = one(*cuts[0])
    for cut in cuts[1:]:
        level = level * one(*cut)
    return level


def centred(rng, extent, deviation, most, cuts=(), kind=jnp.bfloat16):
    factor_of = steps_of(rng, extent, cuts, -0.22, 0.18) if cuts else 1.0
    entries = jax.random.normal(rng, extent, jnp.float32) * deviation * factor_of
    return jnp.minimum(jnp.maximum(entries, -most), most).astype(kind)


def setup_inputs(seed: int = 0) -> dict:
    key_of = jax.random.split(jax.random.key(seed), 11)
    moe_in = centred(key_of[0], (TOKENS, D), 1.0, 6.0, ((0, 128),))
    route_ids = draw_route_ids(jax.random.fold_in(key_of[10], 71), 0)
    route_weights = jnp.clip(jnp.exp(math.log(0.6) - 2.4849067 * jax.random.uniform(key_of[2], (TOKENS, TOPK), jnp.float32) ** steps_of(key_of[2], (TOKENS, TOPK), ((0, 128),), -0.2, 0.2)), 0.05, 0.6)
    w_gate = centred(key_of[3], (EXPERTS, D, H), D ** -0.5, 0.09375, ((0, 128),))
    w_up = centred(key_of[4], (EXPERTS, D, H), D ** -0.5, 0.09375, ((0, 128),))
    w_down = centred(key_of[5], (EXPERTS, H, D), H ** -0.5, 0.1875, ((0, 128),))
    queries = draw_queries(jax.random.fold_in(key_of[10], 71), 0)
    cache_latent = draw_cache_latent(jax.random.fold_in(key_of[10], 71), 0)
    cache_rope = draw_cache_rope(jax.random.fold_in(key_of[10], 71), 0)
    lengths = draw_lengths(jax.random.fold_in(key_of[10], 71), 0)
    return dict(moe_in=moe_in, route_ids=route_ids, route_weights=route_weights, w_gate=w_gate, w_up=w_up, w_down=w_down, queries=queries, cache_latent=cache_latent, cache_rope=cache_rope, lengths=lengths)


score_scale = 192.0 ** -0.5
block_rows = 128


def expert_ffn(inputs, gate_one, up_one, down_one):
    gate_act = jnp.dot(inputs, gate_one, preferred_element_type=jnp.float32)
    up_act = jnp.dot(inputs, up_one, preferred_element_type=jnp.float32)
    hidden_act = (jax.nn.silu(gate_act) * up_act).astype(jnp.bfloat16)
    return jnp.dot(hidden_act, down_one, preferred_element_type=jnp.float32).astype(jnp.bfloat16)


def routed_experts(moe_in, route_ids, route_weights, w_gate, w_up, w_down):
    pair_count = TOKENS * TOPK
    pair_expert = route_ids.reshape(-1).astype(jnp.int32)
    pair_weight = route_weights.reshape(-1)
    ordering = jnp.argsort(pair_expert, stable=True).astype(jnp.int32)
    expert_index = jnp.arange(EXPERTS, dtype=jnp.int32)
    counts_all = jnp.sum((pair_expert[:, None] == expert_index[None, :]).astype(jnp.int32), axis=0, dtype=jnp.int32)
    starts_all = jnp.cumsum(counts_all, dtype=jnp.int32) - counts_all

    def expert_step(expert, total):
        count_here = counts_all[expert]
        start_here = starts_all[expert]
        gate_one = w_gate[expert]
        up_one = w_up[expert]
        down_one = w_down[expert]

        def block_step(block_index, accum):
            offsets = block_index * block_rows + jnp.arange(block_rows, dtype=jnp.int32)
            valid = offsets < count_here
            position = ordering[jnp.minimum(start_here + offsets, pair_count - 1)]
            source_row = position // TOPK
            result = expert_ffn(moe_in[source_row], gate_one, up_one, down_one)
            coeff = jnp.where(valid, pair_weight[position], 0.0)
            return accum.at[source_row].add(coeff[:, None] * result.astype(jnp.float32))

        blocks_here = (count_here + block_rows - 1) // block_rows
        return lax.fori_loop(0, blocks_here, block_step, total)

    total = lax.fori_loop(0, EXPERTS, expert_step, jnp.zeros((TOKENS, D), jnp.float32))
    return total.astype(jnp.bfloat16)


def attend_row(packed):
    query_row, latent_row, rope_row, length_row = packed
    scores = jnp.dot(query_row[:, :KV_RANK], latent_row.T, preferred_element_type=jnp.float32)
    scores = (scores + jnp.dot(query_row[:, KV_RANK:], rope_row, preferred_element_type=jnp.float32)) * score_scale
    positions = jnp.arange(CACHE, dtype=jnp.int32)
    scores = jnp.where(positions[None, :] < length_row, scores, -jnp.inf)
    peak = jnp.max(scores, axis=-1, keepdims=True)
    weights = jnp.exp(scores - peak)
    probs = (weights / jnp.sum(weights, axis=-1, keepdims=True)).astype(jnp.bfloat16)
    return jnp.dot(probs, latent_row, preferred_element_type=jnp.float32).astype(jnp.bfloat16)


def reference(moe_in, route_ids, route_weights, w_gate, w_up, w_down, queries, cache_latent, cache_rope, lengths):
    moe_out = routed_experts(moe_in, route_ids, route_weights, w_gate, w_up, w_down)
    attn_out = lax.map(attend_row, (queries, cache_latent, cache_rope, lengths))
    return (moe_out, attn_out)
```

```python
import functools
import jax
import jax.numpy as jnp
from jax import lax
from jax.experimental import pallas as pl
from jax.experimental.pallas import tpu as pltpu
from jax.sharding import PartitionSpec as P

f32, bf16 = jnp.float32, jnp.bfloat16
score_scale = 192.0 ** (-0.5)
axes = ("node", "local")
SLOTS = 2
QUARTERS = 4
LANE = 128
PER = SLOTS * QUARTERS
VMEM_LIMIT = 42 * 1024 * 1024
PARTS = 4


def tile_of(j, q):
    return slice((j * QUARTERS + q) * LANE, (j * QUARTERS + q + 1) * LANE)


def replicated(per_choice):
    return jnp.concatenate([per_choice] * PER, axis=1)


def slot_members(ids, count):
    lanes = ids.shape[1]
    rows = lanes // PER
    expert = lax.broadcasted_iota(jnp.int32, (count, lanes), 0)
    chosen = [ids[k : k + 1, :] == expert for k in range(ids.shape[0])]
    present = functools.reduce(jnp.logical_or, chosen)
    first = lax.broadcasted_iota(jnp.int32, (lanes, lanes), 0)
    second = lax.broadcasted_iota(jnp.int32, (lanes, lanes), 1)
    before = jnp.logical_and(first // rows == second // rows, first < second).astype(bf16)
    earlier = jnp.dot(present.astype(bf16), before, preferred_element_type=f32)
    slot = (lax.broadcasted_iota(jnp.int32, (count, lanes), 1) // (rows * QUARTERS)).astype(f32)
    return jnp.logical_and(present, earlier == slot), chosen


def at_places(per_expert):
    count, lanes = per_expert.shape
    places = count * PER
    rows = lanes // PER
    place = lax.broadcasted_iota(jnp.int32, (places, count), 0)
    owner = lax.broadcasted_iota(jnp.int32, (places, count), 1)
    widen = (place // PER == owner).astype(bf16)
    wide = jnp.dot(widen, per_expert, preferred_element_type=f32)
    place = lax.broadcasted_iota(jnp.int32, (places, lanes), 0)
    lane = lax.broadcasted_iota(jnp.int32, (places, lanes), 1)
    return jnp.where(place % PER == lane // rows, wide, 0.0)


def pack_kernel(choices, meta_hbm, rows_hbm, send_ref, meta, rows, meta_sem, rows_sem):
    meta_copy = pltpu.make_async_copy(meta_hbm, meta, meta_sem)
    rows_copy = pltpu.make_async_copy(rows_hbm, rows, rows_sem)
    meta_copy.start()
    rows_copy.start()
    width = send_ref.shape[1]
    count = send_ref.shape[0] // PER
    meta_copy.wait()
    members, _ = slot_members(replicated(meta[:choices, :]), count)
    pick = at_places(members.astype(bf16)).astype(bf16)
    rows_copy.wait()
    quarters = jnp.concatenate(
        [
            jnp.concatenate([rows[:, tile_of(j, q)] for j in range(width // LANE)], axis=1)
            for q in range(QUARTERS)
        ]
        * SLOTS,
        axis=0,
    )
    send_ref[...] = jnp.dot(pick, quarters, preferred_element_type=f32).astype(bf16)


def pack(meta, moe_in, choices, count):
    rows, model_width = moe_in.shape
    return pl.pallas_call(
        functools.partial(pack_kernel, choices),
        out_shape=jax.ShapeDtypeStruct((count * PER, model_width // QUARTERS), bf16),
        in_specs=[pl.BlockSpec(memory_space=pltpu.HBM)] * 2,
        out_specs=pl.BlockSpec(memory_space=pltpu.VMEM),
        scratch_shapes=[
            pltpu.VMEM(meta.shape, meta.dtype),
            pltpu.VMEM(moe_in.shape, moe_in.dtype),
            pltpu.SemaphoreType.DMA,
            pltpu.SemaphoreType.DMA,
        ],
        compiler_params=pltpu.CompilerParams(vmem_limit_bytes=16 * 1024 * 1024),
        name="pack_rows",
    )(meta, moe_in)


def coefficient_table(ids, weights, count):
    members, chosen = slot_members(replicated(ids), count)
    weights = replicated(weights)
    weight = functools.reduce(jnp.add, [jnp.where(c, weights[k : k + 1, :], 0.0) for k, c in enumerate(chosen)])
    weight = jnp.where(members, weight, 0.0)
    high = weight.astype(bf16)
    low = (weight - high.astype(f32)).astype(bf16)
    tables = []
    for part in (high, low):
        table = jnp.transpose(at_places(part))
        half = table.shape[0] // SLOTS
        tables.append((table[:half] + table[half:]).astype(bf16))
    return jnp.concatenate(tables, axis=0)


def combine_kernel(coeff_ref, back_ref, out_ref):
    rows = out_ref.shape[0]
    width = back_ref.shape[1]
    total = jnp.dot(coeff_ref[...], back_ref[...], preferred_element_type=f32)
    for q in range(QUARTERS):
        low = (QUARTERS + q) * rows
        value = total[q * rows : (q + 1) * rows] + total[low : low + rows]
        for j in range(width // LANE):
            out_ref[:, tile_of(j, q)] = value[:, j * LANE : (j + 1) * LANE].astype(bf16)


def combine(coeff, back):
    rows = coeff.shape[0] // (2 * QUARTERS)
    return pl.pallas_call(
        combine_kernel,
        out_shape=jax.ShapeDtypeStruct((rows, back.shape[1] * QUARTERS), bf16),
        in_specs=[pl.BlockSpec(memory_space=pltpu.VMEM)] * 2,
        out_specs=pl.BlockSpec(memory_space=pltpu.VMEM),
        compiler_params=pltpu.CompilerParams(vmem_limit_bytes=16 * 1024 * 1024),
        name="combine_rows",
    )(coeff, back)


def attend(queries, latent, rope, length):
    kv_width = latent.shape[1]
    scores = lax.dot_general(
        queries[:, :kv_width], latent, (((1,), (1,)), ((), ())), preferred_element_type=f32
    )
    scores = (scores + jnp.dot(queries[:, kv_width:], rope, preferred_element_type=f32)) * score_scale
    positions = lax.broadcasted_iota(jnp.int32, (1, latent.shape[0]), 1)
    scores = jnp.where(positions < length, scores, -jnp.inf)
    weights = jnp.exp(scores - jnp.max(scores, axis=1, keepdims=True))
    probs = (weights / jnp.sum(weights, axis=1, keepdims=True)).astype(bf16)
    return jnp.dot(probs, latent, preferred_element_type=f32).astype(bf16)


def expert_kernel(
    got_ref, meta_hbm, weights_hbm, queries_hbm, latent_hbm, rope_hbm, gate_hbm, up_hbm, down_hbm,
    send_ref, coeff_ref, attn_ref,
    meta, weights, queries, latent, rope, gate_buf, up_buf, down_buf, wide, rows, hidden, small_sems, sems,
):
    tiles, places, _ = wide.shape
    count = places // PER
    parts, _, part = gate_buf.shape
    chunk = QUARTERS * LANE

    def places_of(s, q):
        return pl.ds(s * QUARTERS + q, count, stride=PER)

    small = [
        pltpu.make_async_copy(source, target, small_sems.at[i])
        for i, (source, target) in enumerate(
            ((meta_hbm, meta), (weights_hbm, weights), (queries_hbm, queries), (rope_hbm, rope), (latent_hbm, latent))
        )
    ]
    pairs = []
    for h in range(parts):
        columns = pl.ds(h * part, part)
        pairs += [(gate_hbm.at[:, columns], gate_buf.at[h]), (up_hbm.at[:, columns], up_buf.at[h])]
    for j in range(tiles):
        pairs.append((down_hbm.at[:, pl.ds(j * chunk, chunk)], down_buf.at[j]))
    queue = [pltpu.make_async_copy(source, target, sems.at[i]) for i, (source, target) in enumerate(pairs)]
    first, second = queue[: 2 * parts], queue[2 * parts :]

    def start(copies):
        for copy in copies:
            copy.start()

    def wait(copies):
        for copy in copies:
            copy.wait()

    start(small + first)
    for j in range(tiles):
        wide[j] = got_ref[:, j * LANE : (j + 1) * LANE].astype(f32)
        for q in range(QUARTERS):
            for s in range(SLOTS):
                rows[s * count : (s + 1) * count, tile_of(j, q)] = wide[j, places_of(s, q), :].astype(bf16)

    wait(small)
    coeff_ref[...] = coefficient_table(meta[: weights.shape[0], :], weights[...], count)
    attn_ref[...] = attend(jnp.transpose(queries[...]), latent[...], rope[...], meta[weights.shape[0] : weights.shape[0] + 1, 0:1])

    wait(first)
    start(second)
    for h in range(parts):
        gate = jnp.dot(rows[...], gate_buf[h], preferred_element_type=f32)
        up = jnp.dot(rows[...], up_buf[h], preferred_element_type=f32)
        hidden[:, h * part : (h + 1) * part] = (gate / (1.0 + jnp.exp(-gate)) * up).astype(bf16)
    wait(second)
    for j in range(tiles):
        result = jnp.dot(hidden[...], down_buf[j], preferred_element_type=f32)
        for q in range(QUARTERS):
            for s in range(SLOTS):
                wide[j, places_of(s, q), :] = result[s * count : (s + 1) * count, q * LANE : (q + 1) * LANE]
        send_ref[:, j * LANE : (j + 1) * LANE] = wide[j].astype(bf16)


def experts(got, meta, route_weights, gate_one, up_one, down_one, queries, latent, rope):
    places, width = got.shape
    heads, kv_width = queries.shape[1], latent.shape[1]
    model_width, hidden_width = gate_one.shape
    batch = SLOTS * places // PER
    vmem = pl.BlockSpec(memory_space=pltpu.VMEM)
    hbm = pl.BlockSpec(memory_space=pltpu.HBM)
    return pl.pallas_call(
        expert_kernel,
        out_shape=[
            jax.ShapeDtypeStruct((places, width), bf16),
            jax.ShapeDtypeStruct((2 * QUARTERS * meta.shape[1], places), bf16),
            jax.ShapeDtypeStruct((heads, kv_width), bf16),
        ],
        in_specs=[vmem, hbm, hbm, hbm, hbm, hbm, hbm, hbm, hbm],
        out_specs=[vmem] * 3,
        scratch_shapes=[
            pltpu.VMEM(meta.shape, meta.dtype),
            pltpu.VMEM(route_weights.shape, route_weights.dtype),
            pltpu.VMEM(queries.shape, queries.dtype),
            pltpu.VMEM(latent.shape, latent.dtype),
            pltpu.VMEM(rope.shape, rope.dtype),
            pltpu.VMEM((PARTS, model_width, hidden_width // PARTS), bf16),
            pltpu.VMEM((PARTS, model_width, hidden_width // PARTS), bf16),
            pltpu.VMEM((width // LANE, hidden_width, QUARTERS * LANE), bf16),
            pltpu.VMEM((width // LANE, places, LANE), f32),
            pltpu.VMEM((batch, model_width), bf16),
            pltpu.VMEM((batch, hidden_width), bf16),
            pltpu.SemaphoreType.DMA((5,)),
            pltpu.SemaphoreType.DMA((2 * PARTS + width // LANE,)),
        ],
        compiler_params=pltpu.CompilerParams(vmem_limit_bytes=VMEM_LIMIT),
        name="experts_and_attention",
    )(got, meta, route_weights, queries, latent, rope, gate_one, up_one, down_one)


def exchange(places):
    return lax.all_to_all(places, axes, split_axis=0, concat_axis=0, tiled=True)


def local(moe_in, route_ids, route_weights, w_gate, w_up, w_down, queries, cache_latent, cache_rope, lengths):
    count = lax.axis_size("node") * lax.axis_size("local")
    choices = route_ids.shape[1]
    filled = jnp.broadcast_to(lengths[:, None], (choices, route_ids.shape[0]))
    meta = jnp.concatenate([route_ids.T, filled], axis=0)
    got = exchange(pack(meta, moe_in, choices, count))
    results, coeff, attn_out = experts(
        got, meta, route_weights.T, w_gate[0], w_up[0], w_down[0], queries[0].T, cache_latent[0], cache_rope[0]
    )
    return combine(coeff, exchange(results)), attn_out[None]


def solution(mesh):
    row, cube = P(axes, None), P(axes, None, None)
    return jax.shard_map(
        local,
        mesh=mesh,
        in_specs=(row, row, row, cube, cube, cube, cube, cube, cube, P(axes)),
        out_specs=(row, cube),
        check_vma=False,
    )
```

```python
import functools
import jax
import jax.numpy as jnp
from jax import lax
from jax.experimental import pallas as pl
from jax.experimental.pallas import tpu as pltpu
from jax.sharding import PartitionSpec as P

f32, bf16 = jnp.float32, jnp.bfloat16
score_scale = 192.0 ** (-0.5)
axes = ("node", "local")
SLOTS = 2
QUARTERS = 4
LANE = 128
PER = SLOTS * QUARTERS
VMEM_LIMIT = 33 * 1024 * 1024
PARTS = 4


def tile_of(j, q):
    return slice((j * QUARTERS + q) * LANE, (j * QUARTERS + q + 1) * LANE)


def replicated(per_choice):
    return jnp.concatenate([per_choice] * PER, axis=1)


def slot_members(ids, count):
    lanes = ids.shape[1]
    rows = lanes // PER
    expert = lax.broadcasted_iota(jnp.int32, (count, lanes), 0)
    chosen = [ids[k : k + 1, :] == expert for k in range(ids.shape[0])]
    present = functools.reduce(jnp.logical_or, chosen)
    first = lax.broadcasted_iota(jnp.int32, (lanes, lanes), 0)
    second = lax.broadcasted_iota(jnp.int32, (lanes, lanes), 1)
    before = jnp.logical_and(first // rows == second // rows, first < second).astype(bf16)
    earlier = jnp.dot(present.astype(bf16), before, preferred_element_type=f32)
    slot = (lax.broadcasted_iota(jnp.int32, (count, lanes), 1) // (rows * QUARTERS)).astype(f32)
    return jnp.logical_and(present, earlier == slot), chosen


def at_places(per_expert):
    count, lanes = per_expert.shape
    places = count * PER
    rows = lanes // PER
    place = lax.broadcasted_iota(jnp.int32, (places, count), 0)
    owner = lax.broadcasted_iota(jnp.int32, (places, count), 1)
    widen = (place // PER == owner).astype(bf16)
    wide = jnp.dot(widen, per_expert, preferred_element_type=f32)
    place = lax.broadcasted_iota(jnp.int32, (places, lanes), 0)
    lane = lax.broadcasted_iota(jnp.int32, (places, lanes), 1)
    return jnp.where(place % PER == lane // rows, wide, 0.0)


def pack_kernel(choices, meta_hbm, rows_hbm, send_ref, meta, rows, meta_sem, rows_sem):
    meta_copy = pltpu.make_async_copy(meta_hbm, meta, meta_sem)
    rows_copy = pltpu.make_async_copy(rows_hbm, rows, rows_sem)
    meta_copy.start()
    rows_copy.start()
    width = send_ref.shape[1]
    count = send_ref.shape[0] // PER
    meta_copy.wait()
    members, _ = slot_members(replicated(meta[:choices, :]), count)
    pick = at_places(members.astype(bf16)).astype(bf16)
    rows_copy.wait()
    quarters = jnp.concatenate(
        [
            jnp.concatenate([rows[:, tile_of(j, q)] for j in range(width // LANE)], axis=1)
            for q in range(QUARTERS)
        ]
        * SLOTS,
        axis=0,
    )
    send_ref[...] = jnp.dot(pick, quarters, preferred_element_type=f32).astype(bf16)


def pack(meta, moe_in, choices, count):
    rows, model_width = moe_in.shape
    return pl.pallas_call(
        functools.partial(pack_kernel, choices),
        out_shape=jax.ShapeDtypeStruct((count * PER, model_width // QUARTERS), bf16),
        in_specs=[pl.BlockSpec(memory_space=pltpu.HBM)] * 2,
        out_specs=pl.BlockSpec(memory_space=pltpu.VMEM),
        scratch_shapes=[
            pltpu.VMEM(meta.shape, meta.dtype),
            pltpu.VMEM(moe_in.shape, moe_in.dtype),
            pltpu.SemaphoreType.DMA,
            pltpu.SemaphoreType.DMA,
        ],
        compiler_params=pltpu.CompilerParams(vmem_limit_bytes=16 * 1024 * 1024),
        cost_estimate=pl.CostEstimate(flops=1 << 36, bytes_accessed=256 << 20, transcendentals=0),
        name="pack_rows",
    )(meta, moe_in)


def coefficient_table(ids, weights, count):
    members, chosen = slot_members(replicated(ids), count)
    weights = replicated(weights)
    weight = functools.reduce(jnp.add, [jnp.where(c, weights[k : k + 1, :], 0.0) for k, c in enumerate(chosen)])
    weight = jnp.where(members, weight, 0.0)
    high = weight.astype(bf16)
    low = (weight - high.astype(f32)).astype(bf16)
    tables = []
    for part in (high, low):
        table = jnp.transpose(at_places(part))
        half = table.shape[0] // SLOTS
        tables.append((table[:half] + table[half:]).astype(bf16))
    return jnp.concatenate(tables, axis=0)


def combine_kernel(coeff_ref, back_ref, out_ref):
    rows = out_ref.shape[0]
    width = back_ref.shape[1]
    total = jnp.dot(coeff_ref[...], back_ref[...], preferred_element_type=f32)
    for q in range(QUARTERS):
        low = (QUARTERS + q) * rows
        value = total[q * rows : (q + 1) * rows] + total[low : low + rows]
        for j in range(width // LANE):
            out_ref[:, tile_of(j, q)] = value[:, j * LANE : (j + 1) * LANE].astype(bf16)


def combine(coeff, back):
    rows = coeff.shape[0] // (2 * QUARTERS)
    return pl.pallas_call(
        combine_kernel,
        out_shape=jax.ShapeDtypeStruct((rows, back.shape[1] * QUARTERS), bf16),
        in_specs=[pl.BlockSpec(memory_space=pltpu.VMEM)] * 2,
        out_specs=pl.BlockSpec(memory_space=pltpu.VMEM),
        compiler_params=pltpu.CompilerParams(vmem_limit_bytes=16 * 1024 * 1024),
        name="combine_rows",
    )(coeff, back)


def attend(queries, latent, rope, length):
    kv_width = latent.shape[1]
    scores = lax.dot_general(
        queries[:, :kv_width], latent, (((1,), (1,)), ((), ())), preferred_element_type=f32
    )
    scores = (scores + jnp.dot(queries[:, kv_width:], rope, preferred_element_type=f32)) * score_scale
    positions = lax.broadcasted_iota(jnp.int32, (1, latent.shape[0]), 1)
    scores = jnp.where(positions < length, scores, -jnp.inf)
    weights = jnp.exp(scores - jnp.max(scores, axis=1, keepdims=True))
    probs = (weights / jnp.sum(weights, axis=1, keepdims=True)).astype(bf16)
    return jnp.dot(probs, latent, preferred_element_type=f32).astype(bf16)


def expert_kernel(
    got_ref, meta_hbm, weights_hbm, queries_hbm, latent_hbm, rope_hbm, gate_ref, up_ref, down_hbm,
    send_ref, coeff_ref, attn_ref,
    meta, weights, queries, latent, rope, down_buf, wide, rows, hidden, small_sems, sems,
):
    tiles, places, _ = wide.shape
    count = places // PER
    part = hidden.shape[1] // PARTS
    chunk = QUARTERS * LANE

    def places_of(s, q):
        return pl.ds(s * QUARTERS + q, count, stride=PER)

    small = [
        pltpu.make_async_copy(source, target, small_sems.at[i])
        for i, (source, target) in enumerate(
            ((meta_hbm, meta), (weights_hbm, weights), (queries_hbm, queries), (rope_hbm, rope), (latent_hbm, latent))
        )
    ]
    downs = [
        pltpu.make_async_copy(down_hbm.at[:, pl.ds(j * chunk, chunk)], down_buf.at[j], sems.at[j]) for j in range(tiles)
    ]

    def start(copies):
        for copy in copies:
            copy.start()

    def wait(copies):
        for copy in copies:
            copy.wait()

    start(small + downs)
    wait(small)
    coeff_ref[...] = coefficient_table(meta[: weights.shape[0], :], weights[...], count)
    attn_ref[...] = attend(jnp.transpose(queries[...]), latent[...], rope[...], meta[weights.shape[0] : weights.shape[0] + 1, 0:1])
    for j in range(tiles):
        wide[j] = got_ref[:, j * LANE : (j + 1) * LANE].astype(f32)
        for q in range(QUARTERS):
            for s in range(SLOTS):
                rows[s * count : (s + 1) * count, tile_of(j, q)] = wide[j, places_of(s, q), :].astype(bf16)

    for h in range(PARTS):
        columns = slice(h * part, (h + 1) * part)
        gate = jnp.dot(rows[...], gate_ref[:, columns], preferred_element_type=f32)
        up = jnp.dot(rows[...], up_ref[:, columns], preferred_element_type=f32)
        hidden[:, columns] = (gate / (1.0 + jnp.exp(-gate)) * up).astype(bf16)
    wait(downs)
    for j in range(tiles):
        result = jnp.dot(hidden[...], down_buf[j], preferred_element_type=f32)
        for q in range(QUARTERS):
            for s in range(SLOTS):
                wide[j, places_of(s, q), :] = result[s * count : (s + 1) * count, q * LANE : (q + 1) * LANE]
        send_ref[:, j * LANE : (j + 1) * LANE] = wide[j].astype(bf16)


def experts(got, meta, route_weights, gate_one, up_one, down_one, queries, latent, rope):
    places, width = got.shape
    heads, kv_width = queries.shape[1], latent.shape[1]
    model_width, hidden_width = gate_one.shape
    batch = SLOTS * places // PER
    vmem = pl.BlockSpec(memory_space=pltpu.VMEM)
    hbm = pl.BlockSpec(memory_space=pltpu.HBM)
    return pl.pallas_call(
        expert_kernel,
        out_shape=[
            jax.ShapeDtypeStruct((places, width), bf16),
            jax.ShapeDtypeStruct((2 * QUARTERS * meta.shape[1], places), bf16),
            jax.ShapeDtypeStruct((heads, kv_width), bf16),
        ],
        in_specs=[vmem, hbm, hbm, hbm, hbm, hbm, vmem, vmem, hbm],
        out_specs=[vmem] * 3,
        scratch_shapes=[
            pltpu.VMEM(meta.shape, meta.dtype),
            pltpu.VMEM(route_weights.shape, route_weights.dtype),
            pltpu.VMEM(queries.shape, queries.dtype),
            pltpu.VMEM(latent.shape, latent.dtype),
            pltpu.VMEM(rope.shape, rope.dtype),
            pltpu.VMEM((width // LANE, hidden_width, QUARTERS * LANE), bf16),
            pltpu.VMEM((width // LANE, places, LANE), f32),
            pltpu.VMEM((batch, model_width), bf16),
            pltpu.VMEM((batch, hidden_width), bf16),
            pltpu.SemaphoreType.DMA((5,)),
            pltpu.SemaphoreType.DMA((width // LANE,)),
        ],
        compiler_params=pltpu.CompilerParams(vmem_limit_bytes=VMEM_LIMIT),
        name="experts_and_attention",
    )(got, meta, route_weights, queries, latent, rope, gate_one, up_one, down_one)


def exchange(places):
    return lax.all_to_all(places, axes, split_axis=0, concat_axis=0, tiled=True)


def local(moe_in, route_ids, route_weights, w_gate, w_up, w_down, queries, cache_latent, cache_rope, lengths):
    count = lax.axis_size("node") * lax.axis_size("local")
    choices = route_ids.shape[1]
    filled = jnp.broadcast_to(lengths[:, None], (choices, route_ids.shape[0]))
    meta = jnp.concatenate([route_ids.T, filled], axis=0)
    got = exchange(pack(meta, moe_in, choices, count))
    results, coeff, attn_out = experts(
        got, meta, route_weights.T, w_gate[0], w_up[0], w_down[0], queries[0].T, cache_latent[0], cache_rope[0]
    )
    return combine(coeff, exchange(results)), attn_out[None]


def solution(mesh):
    row, cube = P(axes, None), P(axes, None, None)
    return jax.shard_map(
        local,
        mesh=mesh,
        in_specs=(row, row, row, cube, cube, cube, cube, cube, cube, P(axes)),
        out_specs=(row, cube),
        check_vma=False,
    )
```

```python
import functools
import jax
import jax.numpy as jnp
from jax import lax
from jax.experimental import pallas as pl
from jax.experimental.pallas import tpu as pltpu
from jax.sharding import PartitionSpec as P

f32, bf16 = jnp.float32, jnp.bfloat16
score_scale = 192.0 ** (-0.5)
LOG2_E = 1.4426950408889634
axes = ("node", "local")
SLOTS = 2
QUARTERS = 4
LANE = 128
PER = SLOTS * QUARTERS
VMEM_LIMIT = 33 * 1024 * 1024
PARTS = 2
UNIT = 64


def tile_of(j, q):
    return slice((j * QUARTERS + q) * LANE, (j * QUARTERS + q + 1) * LANE)


def replicated(per_choice):
    return jnp.concatenate([per_choice] * PER, axis=1)


def slot_members(ids, count):
    lanes = ids.shape[1]
    rows = lanes // PER
    expert = lax.broadcasted_iota(jnp.int32, (count, lanes), 0)
    chosen = [ids[k : k + 1, :] == expert for k in range(ids.shape[0])]
    present = functools.reduce(jnp.logical_or, chosen)
    first = lax.broadcasted_iota(jnp.int32, (lanes, lanes), 0)
    second = lax.broadcasted_iota(jnp.int32, (lanes, lanes), 1)
    before = jnp.logical_and(first // rows == second // rows, first < second).astype(bf16)
    earlier = jnp.dot(present.astype(bf16), before, preferred_element_type=f32)
    slot = (lax.broadcasted_iota(jnp.int32, (count, lanes), 1) // (rows * QUARTERS)).astype(f32)
    return jnp.logical_and(present, earlier == slot), chosen


def at_places(per_expert):
    count, lanes = per_expert.shape
    places = count * PER
    rows = lanes // PER
    place = lax.broadcasted_iota(jnp.int32, (places, count), 0)
    owner = lax.broadcasted_iota(jnp.int32, (places, count), 1)
    widen = (place // PER == owner).astype(bf16)
    wide = jnp.dot(widen, per_expert, preferred_element_type=f32)
    place = lax.broadcasted_iota(jnp.int32, (places, lanes), 0)
    lane = lax.broadcasted_iota(jnp.int32, (places, lanes), 1)
    return jnp.where(place % PER == lane // rows, wide, 0.0)


def facts_of(meta, choices, rows):
    start = meta.shape[0] - 2 * choices
    values = meta[start:, :LANE].astype(f32)
    length = values[choices : choices + 1, 0:1] * UNIT + values[2 * choices - 1 :, 0:1]
    return values[:choices, :rows].astype(jnp.int32), length.astype(jnp.int32)


def pack_kernel(choices, meta_ref, send_ref):
    width = send_ref.shape[1]
    count = send_ref.shape[0] // PER
    rows = meta_ref.shape[0] - 2 * choices
    ids, _ = facts_of(meta_ref, choices, rows)
    members, _ = slot_members(replicated(ids), count)
    pick = at_places(members.astype(bf16)).astype(bf16)
    quarters = jnp.concatenate(
        [
            jnp.concatenate([meta_ref[:rows, tile_of(j, q)] for j in range(width // LANE)], axis=1)
            for q in range(QUARTERS)
        ]
        * SLOTS,
        axis=0,
    )
    send_ref[...] = jnp.dot(pick, quarters, preferred_element_type=f32).astype(bf16)


def pack(meta, rows, choices, count):
    return pl.pallas_call(
        functools.partial(pack_kernel, choices),
        out_shape=jax.ShapeDtypeStruct((count * PER, meta.shape[1] // QUARTERS), bf16),
        in_specs=[pl.BlockSpec(memory_space=pltpu.VMEM)],
        out_specs=pl.BlockSpec(memory_space=pltpu.VMEM),
        compiler_params=pltpu.CompilerParams(vmem_limit_bytes=16 * 1024 * 1024),
        cost_estimate=pl.CostEstimate(flops=1 << 36, bytes_accessed=256 << 20, transcendentals=0),
        name="pack_rows",
    )(meta)


def coefficient_table(ids, weights, count):
    members, chosen = slot_members(replicated(ids), count)
    weights = replicated(weights)
    weight = functools.reduce(jnp.add, [jnp.where(c, weights[k : k + 1, :], 0.0) for k, c in enumerate(chosen)])
    weight = jnp.where(members, weight, 0.0)
    high = weight.astype(bf16)
    low = (weight - high.astype(f32)).astype(bf16)
    tables = []
    for part in (high, low):
        table = jnp.transpose(at_places(part))
        half = table.shape[0] // SLOTS
        tables.append((table[:half] + table[half:]).astype(bf16))
    return jnp.concatenate(tables, axis=0)


def combine_kernel(coeff_ref, back_ref, out_ref):
    rows = out_ref.shape[0]
    width = back_ref.shape[1]
    total = jnp.dot(coeff_ref[...], back_ref[...], preferred_element_type=f32)
    for q in range(QUARTERS):
        low = (QUARTERS + q) * rows
        value = total[q * rows : (q + 1) * rows] + total[low : low + rows]
        for j in range(width // LANE):
            out_ref[:, tile_of(j, q)] = value[:, j * LANE : (j + 1) * LANE].astype(bf16)


def combine(coeff, back):
    rows = coeff.shape[0] // (2 * QUARTERS)
    return pl.pallas_call(
        combine_kernel,
        out_shape=jax.ShapeDtypeStruct((rows, back.shape[1] * QUARTERS), bf16),
        in_specs=[pl.BlockSpec(memory_space=pltpu.VMEM)] * 2,
        out_specs=pl.BlockSpec(memory_space=pltpu.VMEM),
        compiler_params=pltpu.CompilerParams(vmem_limit_bytes=16 * 1024 * 1024),
        name="combine_rows",
    )(coeff, back)


def attend(queries, latent, rope, length):
    kv_width = latent.shape[1]
    scores = lax.dot_general(
        queries[:, :kv_width], latent, (((1,), (1,)), ((), ())), preferred_element_type=f32
    )
    scores = scores + jnp.dot(queries[:, kv_width:], rope, preferred_element_type=f32)
    positions = lax.broadcasted_iota(jnp.int32, (1, latent.shape[0]), 1)
    scores = jnp.where(positions < length, scores, -jnp.inf)
    weights = jnp.exp2((scores - jnp.max(scores, axis=1, keepdims=True)) * (score_scale * LOG2_E))
    total = jnp.sum(weights, axis=1, keepdims=True)
    return (jnp.dot(weights.astype(bf16), latent, preferred_element_type=f32) / total).astype(bf16)


def expert_kernel(
    got_ref, meta_ref, weights_hbm, queries_hbm, latent_hbm, rope_hbm, gate_ref, up_ref, down_hbm,
    send_ref, coeff_ref, attn_ref,
    weights, queries, latent, rope, down_buf, wide, rows, hidden, small_sems, sems,
):
    tiles, places, _ = wide.shape
    count = places // PER
    part = hidden.shape[1] // PARTS
    chunk = QUARTERS * LANE

    def places_of(s, q):
        return pl.ds(s * QUARTERS + q, count, stride=PER)

    small = [
        pltpu.make_async_copy(source, target, small_sems.at[i])
        for i, (source, target) in enumerate(
            ((weights_hbm, weights), (queries_hbm, queries), (rope_hbm, rope), (latent_hbm, latent))
        )
    ]
    downs = [
        pltpu.make_async_copy(down_hbm.at[:, pl.ds(j * chunk, chunk)], down_buf.at[j], sems.at[j]) for j in range(tiles)
    ]

    def start(copies):
        for copy in copies:
            copy.start()

    def wait(copies):
        for copy in copies:
            copy.wait()

    start(small + downs)
    wait(small)
    ids, length = facts_of(meta_ref, *weights.shape)
    coeff_ref[...] = coefficient_table(ids, weights[...], count)
    attn_ref[...] = attend(jnp.transpose(queries[...]), latent[...], rope[...], length)
    for j in range(tiles):
        wide[j] = got_ref[:, j * LANE : (j + 1) * LANE].astype(f32)
        for q in range(QUARTERS):
            for s in range(SLOTS):
                rows[s * count : (s + 1) * count, tile_of(j, q)] = wide[j, places_of(s, q), :].astype(bf16)

    for h in range(PARTS):
        columns = slice(h * part, (h + 1) * part)
        gate = jnp.dot(rows[...], gate_ref[:, columns], preferred_element_type=f32)
        up = jnp.dot(rows[...], up_ref[:, columns], preferred_element_type=f32)
        hidden[:, columns] = (gate * (0.5 + 0.5 * jnp.tanh(0.5 * gate)) * up).astype(bf16)
    wait(downs)
    for j in range(tiles):
        result = jnp.dot(hidden[...], down_buf[j], preferred_element_type=f32)
        for q in range(QUARTERS):
            for s in range(SLOTS):
                wide[j, places_of(s, q), :] = result[s * count : (s + 1) * count, q * LANE : (q + 1) * LANE]
        send_ref[:, j * LANE : (j + 1) * LANE] = wide[j].astype(bf16)


def experts(got, meta, route_weights, gate_one, up_one, down_one, queries, latent, rope):
    places, width = got.shape
    heads, kv_width = queries.shape[1], latent.shape[1]
    model_width, hidden_width = gate_one.shape
    batch = SLOTS * places // PER
    vmem = pl.BlockSpec(memory_space=pltpu.VMEM)
    hbm = pl.BlockSpec(memory_space=pltpu.HBM)
    return pl.pallas_call(
        expert_kernel,
        out_shape=[
            jax.ShapeDtypeStruct((places, width), bf16),
            jax.ShapeDtypeStruct((2 * QUARTERS * route_weights.shape[1], places), bf16),
            jax.ShapeDtypeStruct((heads, kv_width), bf16),
        ],
        in_specs=[vmem, vmem, hbm, hbm, hbm, hbm, vmem, vmem, hbm],
        out_specs=[vmem] * 3,
        scratch_shapes=[
            pltpu.VMEM(route_weights.shape, route_weights.dtype),
            pltpu.VMEM(queries.shape, queries.dtype),
            pltpu.VMEM(latent.shape, latent.dtype),
            pltpu.VMEM(rope.shape, rope.dtype),
            pltpu.VMEM((width // LANE, hidden_width, QUARTERS * LANE), bf16),
            pltpu.VMEM((width // LANE, places, LANE), f32),
            pltpu.VMEM((batch, model_width), bf16),
            pltpu.VMEM((batch, hidden_width), bf16),
            pltpu.SemaphoreType.DMA((4,)),
            pltpu.SemaphoreType.DMA((width // LANE,)),
        ],
        compiler_params=pltpu.CompilerParams(vmem_limit_bytes=VMEM_LIMIT),
        name="experts_and_attention",
    )(got, meta, route_weights, queries, latent, rope, gate_one, up_one, down_one)


def exchange(places):
    return lax.all_to_all(places, axes, split_axis=0, concat_axis=0, tiled=True)


def local(moe_in, route_ids, route_weights, w_gate, w_up, w_down, queries, cache_latent, cache_rope, lengths):
    count = lax.axis_size("node") * lax.axis_size("local")
    choices = route_ids.shape[1]
    rows, model_width = moe_in.shape
    tail = (rows + 2 * choices, model_width)
    row = lax.broadcasted_iota(jnp.int32, tail, 0)
    length = lengths[0]
    facts = jnp.pad(route_ids.T, ((rows, choices), (0, model_width - rows)))
    filled = jnp.where(row < rows + choices + choices // 2, length // UNIT, length % UNIT)
    meta = jnp.pad(moe_in, ((0, 2 * choices), (0, 0)))
    meta = jnp.where(row < rows, meta, jnp.where(row < rows + choices, facts, filled).astype(bf16))
    got = exchange(pack(meta, rows, choices, count))
    results, coeff, attn_out = experts(
        got, meta, route_weights.T, w_gate[0], w_up[0], w_down[0], queries[0].T, cache_latent[0], cache_rope[0]
    )
    return combine(coeff, exchange(results)), attn_out[None]


def solution(mesh):
    row, cube = P(axes, None), P(axes, None, None)
    return jax.shard_map(
        local,
        mesh=mesh,
        in_specs=(row, row, row, cube, cube, cube, cube, cube, cube, P(axes)),
        out_specs=(row, cube),
        check_vma=False,
    )
```

```python
import functools
import jax
import jax.numpy as jnp
from jax import lax
from jax.experimental import pallas as pl
from jax.experimental.pallas import tpu as pltpu
from jax.sharding import PartitionSpec as P

f32, bf16 = jnp.float32, jnp.bfloat16
score_scale = 192.0 ** (-0.5)
LOG2_E = 1.4426950408889634
axes = ("node", "local")
SLOTS = 2
QUARTERS = 4
LANE = 128
PER = SLOTS * QUARTERS
VMEM_LIMIT = 33 * 1024 * 1024
PARTS = 2
UNIT = 64
GROUP = 1


def tile_of(j, q):
    return slice((j * QUARTERS + q) * LANE, (j * QUARTERS + q + 1) * LANE)


def replicated(per_choice):
    return jnp.concatenate([per_choice] * PER, axis=1)


def slot_members(ids, count):
    lanes = ids.shape[1]
    rows = lanes // PER
    expert = lax.broadcasted_iota(jnp.int32, (count, lanes), 0)
    chosen = [ids[k : k + 1, :] == expert for k in range(ids.shape[0])]
    present = functools.reduce(jnp.logical_or, chosen)
    first = lax.broadcasted_iota(jnp.int32, (lanes, lanes), 0)
    second = lax.broadcasted_iota(jnp.int32, (lanes, lanes), 1)
    before = jnp.logical_and(first // rows == second // rows, first < second).astype(bf16)
    earlier = jnp.dot(present.astype(bf16), before, preferred_element_type=f32)
    slot = (lax.broadcasted_iota(jnp.int32, (count, lanes), 1) // (rows * QUARTERS)).astype(f32)
    return jnp.logical_and(present, earlier == slot), chosen


def at_places(per_expert):
    count, lanes = per_expert.shape
    places = count * PER
    rows = lanes // PER
    place = lax.broadcasted_iota(jnp.int32, (places, count), 0)
    owner = lax.broadcasted_iota(jnp.int32, (places, count), 1)
    widen = (place // PER == owner).astype(bf16)
    wide = jnp.dot(widen, per_expert, preferred_element_type=f32)
    place = lax.broadcasted_iota(jnp.int32, (places, lanes), 0)
    lane = lax.broadcasted_iota(jnp.int32, (places, lanes), 1)
    return jnp.where(place % PER == lane // rows, wide, 0.0)


def facts_of(meta, choices, rows):
    start = meta.shape[0] - 2 * choices
    values = meta[start:, :LANE].astype(f32)
    length = values[choices : choices + 1, 0:1] * UNIT + values[2 * choices - 1 :, 0:1]
    return values[:choices, :rows].astype(jnp.int32), length.astype(jnp.int32)


def pack_kernel(choices, meta_ref, send_ref):
    width = send_ref.shape[1]
    count = send_ref.shape[0] // PER
    rows = meta_ref.shape[0] - 2 * choices
    ids, _ = facts_of(meta_ref, choices, rows)
    members, _ = slot_members(replicated(ids), count)
    pick = at_places(members.astype(bf16)).astype(bf16)
    quarters = jnp.concatenate(
        [
            jnp.concatenate([meta_ref[:rows, tile_of(j, q)] for j in range(width // LANE)], axis=1)
            for q in range(QUARTERS)
        ]
        * SLOTS,
        axis=0,
    )
    send_ref[...] = jnp.dot(pick, quarters, preferred_element_type=f32).astype(bf16)


def pack(meta, rows, choices, count):
    return pl.pallas_call(
        functools.partial(pack_kernel, choices),
        out_shape=jax.ShapeDtypeStruct((count * PER, meta.shape[1] // QUARTERS), bf16),
        in_specs=[pl.BlockSpec(memory_space=pltpu.VMEM)],
        out_specs=pl.BlockSpec(memory_space=pltpu.VMEM),
        compiler_params=pltpu.CompilerParams(vmem_limit_bytes=16 * 1024 * 1024),
        cost_estimate=pl.CostEstimate(flops=1 << 36, bytes_accessed=256 << 20, transcendentals=0),
        name="pack_rows",
    )(meta)


def coefficient_table(ids, weights, count):
    members, chosen = slot_members(replicated(ids), count)
    weights = replicated(weights)
    weight = functools.reduce(jnp.add, [jnp.where(c, weights[k : k + 1, :], 0.0) for k, c in enumerate(chosen)])
    weight = jnp.where(members, weight, 0.0)
    high = weight.astype(bf16)
    low = (weight - high.astype(f32)).astype(bf16)
    tables = []
    for part in (high, low):
        table = jnp.transpose(at_places(part))
        half = table.shape[0] // SLOTS
        tables.append((table[:half] + table[half:]).astype(bf16))
    return jnp.concatenate(tables, axis=0)


def combine_kernel(coeff_ref, back_ref, out_ref):
    rows = out_ref.shape[0]
    width = back_ref.shape[1]
    total = jnp.dot(coeff_ref[...], back_ref[...], preferred_element_type=f32)
    for q in range(QUARTERS):
        low = (QUARTERS + q) * rows
        value = total[q * rows : (q + 1) * rows] + total[low : low + rows]
        for j in range(width // LANE):
            out_ref[:, tile_of(j, q)] = value[:, j * LANE : (j + 1) * LANE].astype(bf16)


def combine(coeff, back):
    rows = coeff.shape[0] // (2 * QUARTERS)
    return pl.pallas_call(
        combine_kernel,
        out_shape=jax.ShapeDtypeStruct((rows, back.shape[1] * QUARTERS), bf16),
        in_specs=[pl.BlockSpec(memory_space=pltpu.VMEM)] * 2,
        out_specs=pl.BlockSpec(memory_space=pltpu.VMEM),
        compiler_params=pltpu.CompilerParams(vmem_limit_bytes=16 * 1024 * 1024),
        name="combine_rows",
    )(coeff, back)


def attend(queries, latent, rope, length):
    kv_width = latent.shape[1]
    scores = lax.dot_general(
        queries[:, :kv_width], latent, (((1,), (1,)), ((), ())), preferred_element_type=f32
    )
    scores = scores + jnp.dot(queries[:, kv_width:], rope, preferred_element_type=f32)
    positions = lax.broadcasted_iota(jnp.int32, (1, latent.shape[0]), 1)
    scores = jnp.where(positions < length, scores, -jnp.inf)
    weights = jnp.exp2((scores - jnp.max(scores, axis=1, keepdims=True)) * (score_scale * LOG2_E))
    total = jnp.sum(weights, axis=1, keepdims=True)
    return (jnp.dot(weights.astype(bf16), latent, preferred_element_type=f32) / total).astype(bf16)


def expert_kernel(
    got_ref, meta_ref, weights_hbm, queries_hbm, latent_hbm, rope_hbm, gate_ref, up_ref, down_hbm,
    send_ref, coeff_ref, attn_ref,
    weights, queries, latent, rope, down_buf, wide, rows, hidden, small_sems, sems,
):
    tiles, places, _ = wide.shape
    count = places // PER
    part = hidden.shape[1] // PARTS
    chunk = QUARTERS * LANE

    def places_of(s, q):
        return pl.ds(s * QUARTERS + q, count, stride=PER)

    small = [
        pltpu.make_async_copy(source, target, small_sems.at[i])
        for i, (source, target) in enumerate(
            ((weights_hbm, weights), (queries_hbm, queries), (rope_hbm, rope), (latent_hbm, latent))
        )
    ]
    downs = [pltpu.make_async_copy(down_hbm, down_buf, sems.at[0])]

    def start(copies):
        for copy in copies:
            copy.start()

    def wait(copies):
        for copy in copies:
            copy.wait()

    start(small + downs)
    wait(small)
    ids, length = facts_of(meta_ref, *weights.shape)
    coeff_ref[...] = coefficient_table(ids, weights[...], count)
    attn_ref[...] = attend(jnp.transpose(queries[...]), latent[...], rope[...], length)
    for j in range(tiles):
        wide[j] = got_ref[:, j * LANE : (j + 1) * LANE].astype(f32)
        for q in range(QUARTERS):
            for s in range(SLOTS):
                rows[s * count : (s + 1) * count, tile_of(j, q)] = wide[j, places_of(s, q), :].astype(bf16)

    for h in range(PARTS):
        columns = slice(h * part, (h + 1) * part)
        gate = jnp.dot(rows[...], gate_ref[:, columns], preferred_element_type=f32)
        up = jnp.dot(rows[...], up_ref[:, columns], preferred_element_type=f32)
        hidden[:, columns] = (gate * (0.5 + 0.5 * jnp.tanh(0.5 * gate)) * up).astype(bf16)
    wait(downs)
    for first in range(0, tiles, GROUP):
        last = min(first + GROUP, tiles)
        result = jnp.dot(hidden[...], down_buf[:, first * chunk : last * chunk], preferred_element_type=f32)
        for j in range(first, last):
            for q in range(QUARTERS):
                at = ((j - first) * QUARTERS + q) * LANE
                for s in range(SLOTS):
                    wide[j, places_of(s, q), :] = result[s * count : (s + 1) * count, at : at + LANE]
            send_ref[:, j * LANE : (j + 1) * LANE] = wide[j].astype(bf16)


def experts(got, meta, route_weights, gate_one, up_one, down_one, queries, latent, rope):
    places, width = got.shape
    heads, kv_width = queries.shape[1], latent.shape[1]
    model_width, hidden_width = gate_one.shape
    batch = SLOTS * places // PER
    vmem = pl.BlockSpec(memory_space=pltpu.VMEM)
    hbm = pl.BlockSpec(memory_space=pltpu.HBM)
    return pl.pallas_call(
        expert_kernel,
        out_shape=[
            jax.ShapeDtypeStruct((places, width), bf16),
            jax.ShapeDtypeStruct((2 * QUARTERS * route_weights.shape[1], places), bf16),
            jax.ShapeDtypeStruct((heads, kv_width), bf16),
        ],
        in_specs=[vmem, vmem, hbm, hbm, hbm, hbm, vmem, vmem, hbm],
        out_specs=[vmem] * 3,
        scratch_shapes=[
            pltpu.VMEM(route_weights.shape, route_weights.dtype),
            pltpu.VMEM(queries.shape, queries.dtype),
            pltpu.VMEM(latent.shape, latent.dtype),
            pltpu.VMEM(rope.shape, rope.dtype),
            pltpu.VMEM(down_one.shape, bf16),
            pltpu.VMEM((width // LANE, places, LANE), f32),
            pltpu.VMEM((batch, model_width), bf16),
            pltpu.VMEM((batch, hidden_width), bf16),
            pltpu.SemaphoreType.DMA((4,)),
            pltpu.SemaphoreType.DMA((1,)),
        ],
        compiler_params=pltpu.CompilerParams(vmem_limit_bytes=VMEM_LIMIT),
        name="experts_and_attention",
    )(got, meta, route_weights, queries, latent, rope, gate_one, up_one, down_one)


def exchange(places):
    return lax.all_to_all(places, axes, split_axis=0, concat_axis=0, tiled=True)


def local(moe_in, route_ids, route_weights, w_gate, w_up, w_down, queries, cache_latent, cache_rope, lengths):
    count = lax.axis_size("node") * lax.axis_size("local")
    choices = route_ids.shape[1]
    rows, model_width = moe_in.shape
    tail = (rows + 2 * choices, model_width)
    row = lax.broadcasted_iota(jnp.int32, tail, 0)
    ids = jnp.pad(route_ids.T, ((rows, choices), (0, model_width - rows)))
    length = lengths[:, None]
    units = jnp.pad(length // UNIT, ((rows + choices, choices - 1), (0, model_width - 1)))
    rest = jnp.pad(length % UNIT, ((rows + 2 * choices - 1, 0), (0, model_width - 1)))
    meta = jnp.pad(moe_in, ((0, 2 * choices), (0, 0)))
    meta = jnp.where(row < rows, meta, (ids + units + rest).astype(bf16))
    got = exchange(pack(meta, rows, choices, count))
    results, coeff, attn_out = experts(
        got, meta, route_weights.T, w_gate[0], w_up[0], w_down[0], queries[0].T, cache_latent[0], cache_rope[0]
    )
    return combine(coeff, exchange(results)), attn_out[None]


def solution(mesh):
    row, cube = P(axes, None), P(axes, None, None)
    return jax.shard_map(
        local,
        mesh=mesh,
        in_specs=(row, row, row, cube, cube, cube, cube, cube, cube, P(axes)),
        out_specs=(row, cube),
        check_vma=False,
    )
```
